512 devices in a mesh: box: 128 (over y, z, core), rep: 4 (over x).
Axes of the slice: x: 4, y: 8, z: 8, core: 2. Of those that a mesh axis runs over, the one named last changes fastest.
Arguments:
- multipoles: float32 [121, 32768], P(None, 'box'), may hold values from -6 to 6
- parent_locals: float32 [121, 8192], P(None, ('box', 'rep')), may hold values from -6 to 6
- box_counts: int32 [128], P('box'), may hold values from 128 to 256, as said below
- box_ids: int32 [32768], P('box'), may hold values from 0 to 65534, as said below
- pair_source: int32 [128, 32768], P('rep', 'box'), may hold values from 0 to 1280, as said below
- export_slots: int32 [16384, 32], P('box', 'rep'), may hold values from 0 to 256, as said below
- operators: float32 [128, 14641], P('rep'), may hold values from -0.03125 to 0.03125
- shifters: float32 [8, 14641], replicated, may hold values from -0.5 to 0.5
Outputs:
- local_fields: float32 [121, 32768], P(None, ('box', 'rep'))
The draws below stay inside these ranges and needn't reach their ends.
Inputs may be any that keep to these rules, and one draw needn't show every extreme that they name: `box_counts`: index b of box holds live boxes in its slots 0 to count - 1. `box_ids`: rising within each index of box; index b's ids lie in [2 * 256 b, 2 * 256 (b + 1)), its first a multiple of 8, and the parents (id // 8) of its slots lie within 64 consecutive level-5 ids starting at its first slot's parent. `pair_source`: values below 256 are the device's own slots, other than the target; values from 256 to 256 + 128 * 8 - 1 are entries received from peer e at position j (value 256 + e * 8 + j) and name only filled export positions; the value 256 + 128 * 8 means no partner, and every slot at or beyond the device's count holds it. `export_slots`: filled positions of a row come first and name live slots of the sender; 256 marks an empty position; every row has at least one filled position.
All inputs are finite; a program needn't handle non-finite values.
Results may differ from the reference program's by a relative error of at most 0.0001.
Values sent between devices are 32-bit elements; how exact they have to be, the bound alone decides.
No kernel may reach another device: no remote copies, remote signals or barrier semaphores. Data moves between devices by JAX's collectives and lax.ppermute only.
A program may use at most 64 MiB of HBM per device.

```python
import jax
import jax.numpy as jnp
from jax import lax

ORDER = 10
NCOEF = 121
CLASSES = 128
CAP = 256
SEND = 8
PCAP = 64
NBOX = 32768
N_BOX = 128
N_REP = 4


def shared_loads(key):
    count_key, export_key = jax.random.split(key)
    counts = jax.random.randint(count_key, (N_BOX,), CAP // 2, CAP + 1, dtype=jnp.int32)
    counts = counts.at[0].set(CAP).at[1].set(CAP // 2)
    exports = jax.random.randint(export_key, (N_BOX, N_BOX, N_REP), 1, SEND + 1, dtype=jnp.int32)
    exports = exports.at[0, 0, 0].set(SEND).at[0, 1, 0].set(1)
    return (counts, exports)


def draw_box_counts(key, part):
    counts, exports = shared_loads(key)
    return counts


def draw_box_ids(key, part):
    key = jax.random.fold_in(key, 37)
    gaps = jax.random.randint(key, (N_BOX, CAP), 1, 3, dtype=jnp.int32)
    base = jnp.arange(N_BOX, dtype=jnp.int32)[:, None] * (2 * CAP)
    idents = base + jnp.cumsum(gaps, axis=1) - gaps[:, :1]
    idents = idents.at[:, CAP - 1].set(base[:, 0] + 2 * CAP - 2)
    return idents.reshape(-1).astype(jnp.int32)


def draw_export_slots(key, part):
    counts, exports = shared_loads(key)
    key = jax.random.fold_in(key, 11)
    raw = jax.random.randint(key, (N_BOX, N_BOX, N_REP, SEND), 0, 1 << 30, dtype=jnp.int32)
    chosen = raw % counts[:, None, None, None]
    position = jnp.arange(SEND, dtype=jnp.int32)
    filled = position[None, None, None, :] < exports[:, :, :, None]
    return jnp.where(filled, chosen, CAP).reshape(N_BOX * N_BOX, N_REP * SEND).astype(jnp.int32)


def draw_pair_source(key, part):
    counts, exports = shared_loads(key)
    key = jax.random.fold_in(key, 23)
    kind_key, local_key, peer_key, place_key = jax.random.split(key, 4)
    layout = (CLASSES, N_BOX, CAP)
    kinds = jax.random.randint(kind_key, layout, 0, 10, dtype=jnp.int32)
    owned = counts[None, :, None]
    slot_ids = jnp.arange(CAP, dtype=jnp.int32)[None, None, :]
    stride = jax.random.randint(local_key, layout, 0, 1 << 30, dtype=jnp.int32) % (owned - 1)
    nearby = (slot_ids + 1 + stride) % owned
    peer_ids = jax.random.randint(peer_key, layout, 0, N_BOX, dtype=jnp.int32)
    rep_of = (jnp.arange(CLASSES, dtype=jnp.int32) // (CLASSES // N_REP))[:, None, None]
    box_of = jnp.arange(N_BOX, dtype=jnp.int32)[None, :, None]
    limit = exports[peer_ids, box_of, rep_of]
    place = jax.random.randint(place_key, layout, 0, 1 << 30, dtype=jnp.int32) % limit
    distant = CAP + peer_ids * SEND + place
    dump_entry = CAP + N_BOX * SEND
    chosen = jnp.where(kinds < 3, dump_entry, jnp.where(kinds < 7, nearby, distant))
    chosen = jnp.where(slot_ids < owned, chosen, dump_entry)
    return chosen.reshape(CLASSES, N_BOX * CAP).astype(jnp.int32)


def block_scale(stream_key, shape, pieces, smallest, top_value):
    def one(dim, shards_of):
        steps = jax.random.uniform(jax.random.fold_in(jax.random.fold_in(stream_key, 6), dim), (shards_of,), jnp.float32, smallest / len(pieces), top_value / len(pieces))
        return jnp.repeat(jnp.exp(steps), shape[dim] // shards_of).reshape((-1,) + (1,) * (len(shape) - dim - 1))

    factor_of = one(*pieces[0])
    for cut in pieces[1:]:
        factor_of = factor_of * one(*cut)
    return factor_of


def normal_values(stream_key, extent, deviation, bound, pieces=(), held_as=jnp.bfloat16):
    values = deviation * jax.random.normal(stream_key, extent, jnp.float32)
    if pieces:
        values = values * block_scale(stream_key, extent, pieces, -0.22, 0.18)
    return jnp.clip(values, -bound, bound).astype(held_as)


def setup_inputs(seed: int = 0) -> dict:
    arg_keys = jax.random.split(jax.random.key(seed), 9)
    return {
        "multipoles": normal_values(arg_keys[0], (NCOEF, NBOX), 1.0, 6.0, ((1, 128),), jnp.float32),
        "parent_locals": normal_values(arg_keys[1], (NCOEF, PCAP * N_BOX), 1.0, 6.0, ((1, 512),), jnp.float32),
        "box_counts": draw_box_counts(jax.random.fold_in(arg_keys[8], 71), 0),
        "box_ids": draw_box_ids(jax.random.fold_in(arg_keys[8], 71), 0),
        "pair_source": draw_pair_source(jax.random.fold_in(arg_keys[8], 71), 0),
        "export_slots": draw_export_slots(jax.random.fold_in(arg_keys[8], 71), 0),
        "operators": normal_values(arg_keys[6], (CLASSES, NCOEF * NCOEF), (2 * NCOEF * CLASSES) ** -0.5, 0.03125, ((0, 4),), jnp.float32),
        "shifters": normal_values(arg_keys[7], (8, NCOEF * NCOEF), NCOEF ** -0.5, 0.5, (), jnp.float32),
    }


def degree_parity(length):
    position = jnp.arange(length, dtype=jnp.int32)
    degree = jnp.zeros((length,), jnp.int32)
    for level in range(1, ORDER + 1):
        degree = degree + (position >= level * level).astype(jnp.int32)
    return (1 - 2 * (degree % 2)).astype(jnp.float32)


def reference(multipoles, parent_locals, box_counts, box_ids, pair_source, export_slots, operators, shifters):
    highest = lax.Precision.HIGHEST
    nbox_all = CAP * N_BOX
    cls_dev = CLASSES // N_REP
    slot_ids = jnp.arange(nbox_all, dtype=jnp.int32)
    owner = slot_ids // CAP
    within = slot_ids % CAP
    rep_of = (jnp.arange(CLASSES, dtype=jnp.int32) // cls_dev)[:, None]
    dump_entry = CAP + N_BOX * SEND
    remote = jnp.clip(pair_source - CAP, 0, N_BOX * SEND - 1).astype(jnp.int32)
    peer_ids = remote // SEND
    position = remote % SEND
    exported = export_slots[peer_ids * N_BOX + owner[None, :], rep_of * SEND + position]
    remote_global = jnp.where(exported < CAP, peer_ids * CAP + exported, nbox_all)
    local_global = owner[None, :] * CAP + jnp.minimum(pair_source, CAP - 1)
    partner = jnp.where(pair_source < CAP, local_global,
                        jnp.where(pair_source < dump_entry, remote_global, nbox_all)).astype(jnp.int32)
    parity = degree_parity(NCOEF)
    padded = jnp.concatenate([multipoles, jnp.zeros((NCOEF, 1), jnp.float32)], axis=1)
    signed = multipoles * parity[:, None]
    matrices = operators.reshape(CLASSES, NCOEF, NCOEF)

    def one_class(totals, carried):
        matrix, partners = carried
        forward = jnp.dot(matrix, padded[:, partners], precision=highest, preferred_element_type=jnp.float32)
        mirrored = jnp.dot(matrix, signed, precision=highest, preferred_element_type=jnp.float32) * parity[:, None]
        totals = totals.at[:, :nbox_all].add(forward)
        totals = totals.at[:, partners].add(mirrored)
        return totals, None

    translated, _ = lax.scan(one_class, jnp.zeros((NCOEF, nbox_all + 1), jnp.float32), (matrices, partner))
    grid_ids = box_ids.reshape(N_BOX, CAP)
    parent_slot = (grid_ids // 8 - grid_ids[:, :1] // 8
                   + jnp.arange(N_BOX, dtype=jnp.int32)[:, None] * PCAP).reshape(-1).astype(jnp.int32)
    octant = box_ids % 8
    fathers = parent_locals[:, parent_slot]
    shift_mats = shifters.reshape(8, NCOEF, NCOEF)
    shifted = jnp.zeros((NCOEF, nbox_all), jnp.float32)
    for corner in range(8):
        moved = jnp.dot(shift_mats[corner], fathers, precision=highest, preferred_element_type=jnp.float32)
        shifted = shifted + jnp.where((octant == corner)[None, :], moved, 0.0)
    occupied = within < box_counts[owner]
    return jnp.where(occupied[None, :], translated[:, :nbox_all] + shifted, 0.0)
```

```python
import jax
import jax.numpy as jnp
from jax import lax
from jax.experimental import pallas as pl
from jax.experimental.pallas import tpu as pltpu
from jax.sharding import PartitionSpec as P

ORDER = 10
SEND = 8
Z_BITS = 3
Z_CHIPS = 1 << Z_BITS
LANES = 128
BF = jnp.bfloat16
F32 = jnp.float32
VMEM_LIMIT = 24 * 1024 * 1024


def mm(a, b):
    return jnp.dot(a, b, preferred_element_type=F32)


def split_hl(x):
    hi = x.astype(BF)
    lo = (x - hi.astype(F32)).astype(BF)
    return jnp.concatenate([hi, lo], axis=1)


def fold(x):
    half = x.shape[1] // 2
    return x[:, :half] + x[:, half:]


def parity_lanes(rows):
    k = lax.broadcasted_iota(jnp.int32, (rows, LANES), 1)
    degree = jnp.zeros((rows, LANES), jnp.int32)
    for level in range(1, ORDER + 1):
        degree = degree + jnp.where(k >= level * level, 1, 0)
    return jnp.where((degree & 1) == 0, 1.0, -1.0).astype(F32)


def onehot(mask):
    return jnp.where(mask, 1.0, 0.0).astype(BF)


def matrices_to_rows(src, first, coeffs, out):
    total = coeffs * coeffs
    lane = lax.broadcasted_iota(jnp.int32, (8, LANES), 1)
    for j in range(coeffs):
        base = j * coeffs // LANES * LANES
        shift = j * coeffs - base
        stop = min(base + 2 * LANES, total)
        wide = src[pl.ds(first, 8), base:stop]
        if stop < base + 2 * LANES:
            wide = jnp.concatenate([wide, jnp.zeros((8, base + 2 * LANES - stop), F32)], axis=1)
        if shift:
            wide = pltpu.roll(wide, 2 * LANES - shift, 1)
        row = jnp.where(lane < coeffs, wide[:, :LANES], 0.0)
        out[pl.ds(first * LANES + j, 8, stride=LANES), :] = row
    for j in range(coeffs, LANES):
        out[pl.ds(first * LANES + j, 8, stride=LANES), :] = jnp.zeros((8, LANES), F32)


def chip_ranks(chips):
    rows = chips // Z_CHIPS
    return [((r // Z_CHIPS + r) % Z_CHIPS % rows) * Z_CHIPS + r % Z_CHIPS for r in range(chips)]


def rank_columns(ex, core):
    nb = ex.shape[1]
    rows = nb // 2 // Z_CHIPS
    source = lax.broadcasted_iota(jnp.int32, (nb, nb), 0)
    place = lax.broadcasted_iota(jnp.int32, (nb, nb), 1)
    rank = place >> 1
    z = rank & (Z_CHIPS - 1)
    y = (lax.shift_right_logical(rank, Z_BITS) + z) & (rows - 1)
    column = ((y * Z_CHIPS + z) << 1) | ((place & 1) ^ core)
    wide = jnp.concatenate([ex, ex], axis=0).astype(F32).astype(BF)
    return mm(wide, onehot(source == column))[: ex.shape[0]].astype(jnp.int32)


def far_order(ps, slots, nb, core):
    rows = nb // 2 // Z_CHIPS
    entry = ps - slots
    peer = entry >> 3
    z = (peer >> 1) & (Z_CHIPS - 1)
    y = peer >> (1 + Z_BITS)
    rank = ((y - z) & (rows - 1)) * Z_CHIPS + z
    moved = (((rank << 1) | ((peer & 1) ^ core)) << 3) | (entry & (SEND - 1))
    return jnp.where((entry >= 0) & (entry < nb * SEND), slots + moved, ps)


def spread_rows(row, rows):
    tile = jnp.broadcast_to(row, (16, row.shape[1])).astype(F32).astype(BF)
    return jnp.concatenate([tile] * (rows // 16), axis=0)


def pick16(mask):
    return jnp.where(mask, jnp.ones((), BF), jnp.zeros((), BF))


def export_kernel(
    core_ref, mult_in, ex_in, keep_ref, give_ref, mrow_ref, mult_ref, ex_ref, all_ref, mult_sem, ex_sem
):
    fetch_mult = pltpu.make_async_copy(mult_in, mult_ref, mult_sem)
    fetch_ex = pltpu.make_async_copy(ex_in, ex_ref, ex_sem)
    fetch_mult.start()
    fetch_ex.start()
    fetch_ex.wait()
    coeffs, slots = mult_ref.shape
    nb = ex_ref.shape[1]
    ex = rank_columns(ex_ref[...], core_ref[0])
    ex = jnp.concatenate([ex, jnp.zeros((LANES - SEND, nb), jnp.int32)], axis=0).T
    fetch_mult.wait()
    wide = jnp.concatenate([mult_ref[...], jnp.zeros((LANES - coeffs, slots), F32)], axis=0)
    rows = wide.T
    mrow_ref[...] = rows
    table = split_hl(rows)
    lane = lax.broadcasted_iota(jnp.int32, (nb, slots), 1)
    for j in range(SEND):
        picked = mm(onehot(lane == ex[:, j : j + 1]), table)
        all_ref[pl.ds(j, nb, stride=SEND), :] = fold(picked)
    pairs = all_ref[...].reshape(nb // 2, 2 * SEND, LANES)
    keep_ref[...] = pairs[:, :SEND, :]
    give_ref[...] = pairs[:, SEND:, :]


def reverse_kernel(
    core_ref,
    op_in,
    mrow_ref,
    ps_ref,
    w_out,
    own_ref,
    keep_ref,
    give_ref,
    op_ref,
    t_ref,
    w_ref,
    acc_ref,
    op_sem,
    w_sem,
):
    classes = op_ref.shape[0]
    coeffs = 121
    slots = mrow_ref.shape[0]
    columns = acc_ref.shape[0]
    group = 8
    block = 256

    def fetch(k):
        rows = pl.ds(pl.multiple_of(k * 8, 8), 8)
        return pltpu.make_async_copy(op_in.at[rows, :], op_ref.at[rows, :], op_sem.at[k])

    for k in range(classes // 8):
        fetch(k).start()

    @pl.loop(0, classes // 8)
    def _(k):
        fetch(k).wait()
        matrices_to_rows(op_ref, pl.multiple_of(k * 8, 8), coeffs, t_ref)

    sign = parity_lanes(slots)
    moments = split_hl(mrow_ref[...] * sign)
    acc_ref[...] = jnp.zeros_like(acc_ref)
    row_id = lax.broadcasted_iota(jnp.int32, (block, slots), 0).astype(F32).astype(BF)

    @pl.loop(0, classes // group)
    def _(g):
        mirrors = []
        for i in range(group):
            c = g * group + i
            w = split_hl(t_ref[pl.ds(pl.multiple_of(c * LANES, LANES), LANES), :].T)
            w_ref[c] = w
            mirrors.append(split_hl(fold(mm(moments, jnp.concatenate([w, w], axis=0)))))
        m = jnp.concatenate(mirrors, axis=0)
        ps = ps_ref[pl.ds(pl.multiple_of(g * group, group), group), :]
        ps = far_order(ps, slots, (columns - slots) // SEND, core_ref[0])
        for start in range(0, columns, block):
            here = ps - start
            hot = jnp.concatenate(
                [pick16(row_id == spread_rows(here[i : i + 1, :], block)) for i in range(group)],
                axis=1,
            )
            acc_ref[start : start + block, :] += mm(hot, m)

    copy = pltpu.make_async_copy(w_ref, w_out, w_sem)
    copy.start()
    own_ref[...] = fold(acc_ref[:slots, :]) * sign
    far = columns - slots
    sums = fold(acc_ref[slots:, :]) * parity_lanes(far)
    pairs = sums.reshape(far // (2 * SEND), 2 * SEND, LANES)
    keep_ref[...] = pairs[:, :SEND, :]
    give_ref[...] = pairs[:, SEND:, :]
    copy.wait()


def forward_kernel(
    rep_ref,
    core_ref,
    w_in,
    mrow_ref,
    arr_ref,
    ps_ref,
    ids_ref,
    par_ref,
    sh_ref,
    own_ref,
    out_ref,
    w_ref,
    table_ref,
    cols_ref,
    u_ref,
    acc_ref,
    w_sem,
):
    copy = pltpu.make_async_copy(w_in, w_ref, w_sem)
    copy.start()
    classes = w_ref.shape[0]
    slots = mrow_ref.shape[0]
    columns = table_ref.shape[0]
    coeffs = 121
    block = 256
    table_ref[:slots, :] = split_hl(mrow_ref[...])
    table_ref[slots:, :] = split_hl(arr_ref[...])
    ps = far_order(ps_ref[...], slots, (columns - slots) // SEND, core_ref[0])
    pst = jnp.concatenate([ps, jnp.zeros((LANES - classes, slots), jnp.int32)], axis=0).T
    for c in range(classes):
        cols_ref[c] = jnp.broadcast_to(pst[:, c : c + 1], (slots, LANES))

    acc_ref[...] = jnp.zeros_like(acc_ref)
    lane = lax.broadcasted_iota(jnp.int32, (slots, block), 1).astype(F32).astype(BF)
    group = 4
    copy.wait()

    @pl.loop(0, classes // group)
    def _(g):
        hots = []
        for i in range(group):
            col = cols_ref[g * group + i]
            parts = []
            for start in range(0, columns, block):
                here = (col - start).astype(F32).astype(BF)
                parts.append(pick16(lane == jnp.concatenate([here] * (block // LANES), axis=1)))
            hots.append(jnp.concatenate(parts, axis=1))
        picked = mm(jnp.concatenate(hots, axis=0), table_ref[...]).astype(BF)
        total = None
        for i in range(group):
            w = w_ref[g * group + i]
            part = mm(picked[i * slots : (i + 1) * slots], jnp.concatenate([w, w], axis=0))
            total = part if total is None else total + part
        acc_ref[...] += total

    matrices_to_rows(sh_ref, 0, coeffs, u_ref)
    parents = par_ref[...]
    held = parents.shape[0]
    parents = jnp.concatenate([parents, jnp.zeros((held, LANES - coeffs), F32)], axis=1)
    lhs = split_hl(parents)
    moved = []
    for o in range(8):
        w = split_hl(u_ref[o * LANES : (o + 1) * LANES, :].T)
        moved.append(fold(mm(lhs, jnp.concatenate([w, w], axis=0))))
    moved = split_hl(jnp.concatenate(moved, axis=0))
    ids = jnp.broadcast_to(ids_ref[...], (8, slots))
    parent = lax.shift_right_logical(ids, 3)
    q = parent - parent[:, 0:1] - rep_ref[0] * held
    code = jnp.where((q >= 0) & (q < held), (ids & 7) * held + q, -1)
    code = jnp.concatenate([code, jnp.zeros((LANES - 8, slots), jnp.int32)], axis=0).T
    pick = lax.broadcasted_iota(jnp.int32, (slots, 8 * held), 1)
    shifted = fold(mm(onehot(pick == code[:, 0:1]), moved))
    out_ref[...] = fold(acc_ref[...]) + own_ref[...] + shifted


def landing_kernel(core_ref, cnt_ref, ex_ref, ret_ref, part_ref, out_ref):
    slots = part_ref.shape[0]
    nb = ex_ref.shape[1]
    row = lax.broadcasted_iota(jnp.int32, (slots, nb), 0)
    ex = rank_columns(ex_ref[...], core_ref[0])
    hots = [onehot(row == ex[j : j + 1, :]) for j in range(SEND)]
    vals = [split_hl(ret_ref[pl.ds(j, nb, stride=SEND), :]) for j in range(SEND)]
    landed = fold(mm(jnp.concatenate(hots, axis=1), jnp.concatenate(vals, axis=0)))
    slot = lax.broadcasted_iota(jnp.int32, (slots, LANES), 0)
    out_ref[...] = jnp.where(slot < cnt_ref[0], part_ref[...] + landed, 0.0)


def call(
    kernel, out_shape, n_in, scalars=0, scratch=(), n_out=1, far=(), flops=10**8, moved=10**6
):
    vmem = pl.BlockSpec(memory_space=pltpu.VMEM)
    smem = pl.BlockSpec(memory_space=pltpu.SMEM)
    hbm = pl.BlockSpec(memory_space=pltpu.HBM)
    specs = [smem] * scalars + [vmem] * (n_in - scalars + n_out)
    shapes = list(out_shape) if n_out > 1 else [out_shape]
    for place in far:
        specs[place] = hbm
        if place >= n_in:
            old = shapes[place - n_in]
            shapes[place - n_in] = pltpu.HBM(old.shape, old.dtype)
    made = pl.pallas_call(
        kernel,
        out_shape=shapes if n_out > 1 else shapes[0],
        in_specs=specs[:n_in],
        out_specs=specs[n_in:] if n_out > 1 else specs[n_in],
        scratch_shapes=list(scratch),
        compiler_params=pltpu.CompilerParams(vmem_limit_bytes=VMEM_LIMIT),
        cost_estimate=pl.CostEstimate(flops=flops, bytes_accessed=moved, transcendentals=0),
    )

    def run(*args):
        placed = [
            pltpu.with_memory_space_constraint(x, pltpu.HBM) if i in far else x
            for i, x in enumerate(args)
        ]
        return made(*placed)

    return run


def sds(shape, dtype=F32):
    return jax.ShapeDtypeStruct(shape, dtype)


def across_chips(keep, give, later):
    nb = lax.axis_size("box")
    got = lax.ppermute(give, "box", [(i, i ^ 1) for i in range(nb)])
    both, later = lax.optimization_barrier((jnp.concatenate([keep, got], axis=1), later))
    groups = [[2 * chip + k for chip in chip_ranks(nb // 2)] for k in range(2)]
    landed = lax.all_to_all(
        both, "box", split_axis=0, concat_axis=0, axis_index_groups=groups, tiled=True
    )
    return landed.reshape(nb * SEND, LANES), later


def on_device(
    multipoles, parent_locals, box_counts, box_ids, pair_source, export_slots, operators, shifters
):
    coeffs, slots = multipoles.shape
    classes = operators.shape[0]
    nb = export_slots.shape[0]
    quarters = lax.axis_size("rep")
    quarter = slots // quarters
    sent = nb * SEND
    columns = slots + sent
    heavy = 2 * classes * slots * 2 * LANES * (columns + 2 * LANES)
    ex = export_slots.T
    core = (lax.axis_index("box") & 1).astype(jnp.int32).reshape(1)
    rep = lax.axis_index("rep").astype(jnp.int32).reshape(1)
    row = sds((slots, LANES))
    half = sds((nb // 2, SEND, LANES))
    wide = (classes, LANES, 2 * LANES)
    keep, give, mrow = call(
        export_kernel,
        [half, half, row],
        3,
        scalars=1,
        n_out=3,
        far=(1, 2),
        scratch=[
            pltpu.VMEM(multipoles.shape, F32),
            pltpu.VMEM(ex.shape, jnp.int32),
            pltpu.VMEM((sent, LANES), F32),
            pltpu.SemaphoreType.DMA,
            pltpu.SemaphoreType.DMA,
        ],
    )(core, multipoles, ex)
    arrived, mrow = across_chips(keep, give, mrow)
    w, own, keep, give = call(
        reverse_kernel,
        [sds(wide, BF), row, half, half],
        4,
        scalars=1,
        scratch=[
            pltpu.VMEM(operators.shape, F32),
            pltpu.VMEM((classes * LANES, LANES), F32),
            pltpu.VMEM(wide, BF),
            pltpu.VMEM((columns, 2 * LANES), F32),
            pltpu.SemaphoreType.DMA((classes // 8,)),
            pltpu.SemaphoreType.DMA,
        ],
        n_out=4,
        far=(1, 4),
        flops=heavy,
        moved=4 * operators.size,
    )(core, operators, mrow, pair_source)
    returned, own = across_chips(keep, give, own)
    part = call(
        forward_kernel,
        row,
        10,
        scalars=2,
        far=(2,),
        scratch=[
            pltpu.VMEM(wide, BF),
            pltpu.VMEM((columns, 2 * LANES), BF),
            pltpu.VMEM((classes, slots, LANES), jnp.int32),
            pltpu.VMEM((8 * LANES, LANES), F32),
            pltpu.VMEM((slots, 2 * LANES), F32),
            pltpu.SemaphoreType.DMA,
        ],
        flops=heavy,
        moved=4 * operators.size,
    )(rep, core, w, mrow, arrived, pair_source, box_ids.reshape(1, slots), parent_locals.T, shifters, own)
    summed = call(landing_kernel, row, 5, scalars=2)(core, box_counts, ex, returned, part)
    shares = lax.all_to_all(
        summed.reshape(quarters, quarter, LANES), "rep", split_axis=0, concat_axis=0, tiled=True
    )
    return jnp.sum(shares, axis=0)[:, :coeffs].T


def solution(mesh):
    return jax.shard_map(
        on_device,
        mesh=mesh,
        in_specs=(
            P(None, "box"),
            P(None, ("box", "rep")),
            P("box"),
            P("box"),
            P("rep", "box"),
            P("box", "rep"),
            P("rep", None),
            P(),
        ),
        out_specs=P(None, ("box", "rep")),
        check_vma=False,
    )
```

```python
import jax
import jax.numpy as jnp
from jax import lax
from jax.experimental import pallas as pl
from jax.experimental.pallas import tpu as pltpu
from jax.sharding import PartitionSpec as P

ORDER = 10
SEND = 8
Z_BITS = 3
LANES = 128
BF = jnp.bfloat16
F32 = jnp.float32
VMEM_LIMIT = 24 * 1024 * 1024


def mm(a, b):
    return jnp.dot(a, b, preferred_element_type=F32)


def split_hl(x):
    hi = x.astype(BF)
    lo = (x - hi.astype(F32)).astype(BF)
    return jnp.concatenate([hi, lo], axis=1)


def fold(x):
    half = x.shape[1] // 2
    return x[:, :half] + x[:, half:]


def parity_lanes(rows):
    k = lax.broadcasted_iota(jnp.int32, (rows, LANES), 1)
    degree = jnp.zeros((rows, LANES), jnp.int32)
    for level in range(1, ORDER + 1):
        degree = degree + jnp.where(k >= level * level, 1, 0)
    return jnp.where((degree & 1) == 0, 1.0, -1.0).astype(F32)


def onehot(mask):
    return jnp.where(mask, 1.0, 0.0).astype(BF)


def matrices_to_rows(src, first, coeffs, out):
    total = coeffs * coeffs
    lane = lax.broadcasted_iota(jnp.int32, (8, LANES), 1)
    for j in range(coeffs):
        base = j * coeffs // LANES * LANES
        shift = j * coeffs - base
        stop = min(base + 2 * LANES, total)
        wide = src[pl.ds(first, 8), base:stop]
        if stop < base + 2 * LANES:
            wide = jnp.concatenate([wide, jnp.zeros((8, base + 2 * LANES - stop), F32)], axis=1)
        if shift:
            wide = pltpu.roll(wide, 2 * LANES - shift, 1)
        row = jnp.where(lane < coeffs, wide[:, :LANES], 0.0)
        out[pl.ds(first * LANES + j, 8, stride=LANES), :] = row
    for j in range(coeffs, LANES):
        out[pl.ds(first * LANES + j, 8, stride=LANES), :] = jnp.zeros((8, LANES), F32)


def chip_side(chip):
    return (chip ^ (chip >> Z_BITS)) & 1


def swap_cores(ex, group):
    nb = ex.shape[1]
    lane = lax.broadcasted_iota(jnp.int32, ex.shape, 1)
    swapped = jnp.where((lane & 1) == 0, pltpu.roll(ex, nb - 1, 1), pltpu.roll(ex, 1, 1))
    return jnp.where((chip_side(lane >> 1) ^ group) == 1, swapped, ex)


def far_order(ps, slots, group):
    swapped = chip_side((ps - slots) >> 4) ^ group
    return ps ^ jnp.where(ps >= slots, SEND * swapped, 0)


def spread_rows(row, rows):
    tile = jnp.broadcast_to(row, (16, row.shape[1])).astype(F32).astype(BF)
    return jnp.concatenate([tile] * (rows // 16), axis=0)


def pick16(mask):
    return jnp.where(mask, jnp.ones((), BF), jnp.zeros((), BF))


def export_kernel(
    mult_in, ex_in, out, mrow_ref, mult_ref, ex_ref, cols_ref, sent_ref, mult_sem, ex_sem, out_sem
):
    fetch_mult = pltpu.make_async_copy(mult_in, mult_ref, mult_sem)
    fetch_ex = pltpu.make_async_copy(ex_in, ex_ref, ex_sem)
    fetch_mult.start()
    fetch_ex.start()
    fetch_ex.wait()
    coeffs, slots = mult_ref.shape
    nb = ex_ref.shape[1]
    sent = nb * SEND
    ex = jnp.concatenate([ex_ref[...], jnp.zeros((LANES - SEND, nb), jnp.int32)], axis=0).T
    for j in range(SEND):
        cols_ref[pl.ds(j, nb, stride=SEND), :] = jnp.broadcast_to(ex[:, j : j + 1], (nb, LANES))
    fetch_mult.wait()
    wide = jnp.concatenate([mult_ref[...], jnp.zeros((LANES - coeffs, slots), F32)], axis=0)
    rows = wide.T
    mrow_ref[...] = rows
    table = split_hl(rows)
    block = 256
    lane = lax.broadcasted_iota(jnp.int32, (block, LANES), 1)
    copies = []
    for n in range(sent // block):
        here = pl.ds(n * block, block)
        col = cols_ref[here, :]
        hot = jnp.concatenate([onehot(lane == col - s) for s in range(0, slots, LANES)], axis=1)
        sent_ref[here, :] = fold(mm(hot, table))
        copies.append(pltpu.make_async_copy(sent_ref.at[here, :], out.at[here, :], out_sem.at[n]))
        copies[n].start()
    for copy in copies:
        copy.wait()


def reverse_kernel(
    group_ref,
    op_in,
    mrow_ref,
    ps_ref,
    w_out,
    own_ref,
    keep_ref,
    give_ref,
    op_ref,
    t_ref,
    w_ref,
    acc_ref,
    op_sem,
    w_sem,
):
    classes = op_ref.shape[0]
    coeffs = 121
    slots = mrow_ref.shape[0]
    columns = acc_ref.shape[0]
    step = 8
    block = 256

    def fetch(k):
        rows = pl.ds(pl.multiple_of(k * 8, 8), 8)
        return pltpu.make_async_copy(op_in.at[rows, :], op_ref.at[rows, :], op_sem.at[k])

    for k in range(classes // 8):
        fetch(k).start()

    @pl.loop(0, classes // 8)
    def _(k):
        fetch(k).wait()
        matrices_to_rows(op_ref, pl.multiple_of(k * 8, 8), coeffs, t_ref)

    sign = parity_lanes(slots)
    moments = split_hl(mrow_ref[...] * sign)
    acc_ref[...] = jnp.zeros_like(acc_ref)
    row_id = lax.broadcasted_iota(jnp.int32, (block, slots), 0).astype(F32).astype(BF)

    @pl.loop(0, classes // step)
    def _(g):
        mirrors = []
        for i in range(step):
            c = g * step + i
            w = split_hl(t_ref[pl.ds(pl.multiple_of(c * LANES, LANES), LANES), :].T)
            w_ref[c] = w
            mirrors.append(split_hl(fold(mm(moments, jnp.concatenate([w, w], axis=0)))))
        m = jnp.concatenate(mirrors, axis=0)
        ps = ps_ref[pl.ds(pl.multiple_of(g * step, step), step), :]
        ps = far_order(ps, slots, group_ref[0])
        for start in range(0, columns, block):
            here = ps - start
            hot = jnp.concatenate(
                [pick16(row_id == spread_rows(here[i : i + 1, :], block)) for i in range(step)],
                axis=1,
            )
            acc_ref[start : start + block, :] += mm(hot, m)

    copy = pltpu.make_async_copy(w_ref, w_out, w_sem)
    copy.start()
    own_ref[...] = fold(acc_ref[:slots, :]) * sign
    far = columns - slots
    sums = fold(acc_ref[slots:, :]) * parity_lanes(far)
    pairs = sums.reshape(far // (2 * SEND), 2 * SEND, LANES)
    keep_ref[...] = pairs[:, :SEND, :]
    give_ref[...] = pairs[:, SEND:, :]
    copy.wait()


def forward_kernel(
    rep_ref,
    w_in,
    mrow_ref,
    arr_ref,
    ps_ref,
    ids_ref,
    par_ref,
    sh_ref,
    own_ref,
    out_ref,
    w_ref,
    table_ref,
    cols_ref,
    u_ref,
    acc_ref,
    w_sem,
):
    copy = pltpu.make_async_copy(w_in, w_ref, w_sem)
    copy.start()
    classes = w_ref.shape[0]
    slots = mrow_ref.shape[0]
    columns = table_ref.shape[0]
    coeffs = 121
    block = 256
    table_ref[:slots, :] = split_hl(mrow_ref[...])
    table_ref[slots:, :] = split_hl(arr_ref[...])
    ps = ps_ref[...]
    pst = jnp.concatenate([ps, jnp.zeros((LANES - classes, slots), jnp.int32)], axis=0).T
    for c in range(classes):
        cols_ref[c] = jnp.broadcast_to(pst[:, c : c + 1], (slots, LANES))

    acc_ref[...] = jnp.zeros_like(acc_ref)
    lane = lax.broadcasted_iota(jnp.int32, (slots, block), 1).astype(F32).astype(BF)
    group = 4
    copy.wait()

    @pl.loop(0, classes // group)
    def _(g):
        hots = []
        for i in range(group):
            col = cols_ref[g * group + i]
            parts = []
            for start in range(0, columns, block):
                here = (col - start).astype(F32).astype(BF)
                parts.append(pick16(lane == jnp.concatenate([here] * (block // LANES), axis=1)))
            hots.append(jnp.concatenate(parts, axis=1))
        picked = mm(jnp.concatenate(hots, axis=0), table_ref[...]).astype(BF)
        total = None
        for i in range(group):
            w = w_ref[g * group + i]
            part = mm(picked[i * slots : (i + 1) * slots], jnp.concatenate([w, w], axis=0))
            total = part if total is None else total + part
        acc_ref[...] += total

    matrices_to_rows(sh_ref, 0, coeffs, u_ref)
    parents = par_ref[...]
    held = parents.shape[0]
    parents = jnp.concatenate([parents, jnp.zeros((held, LANES - coeffs), F32)], axis=1)
    lhs = split_hl(parents)
    moved = []
    for o in range(8):
        w = split_hl(u_ref[o * LANES : (o + 1) * LANES, :].T)
        moved.append(fold(mm(lhs, jnp.concatenate([w, w], axis=0))))
    moved = split_hl(jnp.concatenate(moved, axis=0))
    ids = jnp.broadcast_to(ids_ref[...], (8, slots))
    parent = lax.shift_right_logical(ids, 3)
    q = parent - parent[:, 0:1] - rep_ref[0] * held
    code = jnp.where((q >= 0) & (q < held), (ids & 7) * held + q, -1)
    code = jnp.concatenate([code, jnp.zeros((LANES - 8, slots), jnp.int32)], axis=0).T
    pick = lax.broadcasted_iota(jnp.int32, (slots, 8 * held), 1)
    shifted = fold(mm(onehot(pick == code[:, 0:1]), moved))
    out_ref[...] = fold(acc_ref[...]) + own_ref[...] + shifted


def landing_kernel(group_ref, cnt_ref, ex_ref, ret_ref, part_ref, out_ref):
    slots = part_ref.shape[0]
    nb = ex_ref.shape[1]
    row = lax.broadcasted_iota(jnp.int32, (slots, nb), 0)
    ex = swap_cores(ex_ref[...], group_ref[0])
    hots = [onehot(row == ex[j : j + 1, :]) for j in range(SEND)]
    vals = [split_hl(ret_ref[pl.ds(j, nb, stride=SEND), :]) for j in range(SEND)]
    landed = fold(mm(jnp.concatenate(hots, axis=1), jnp.concatenate(vals, axis=0)))
    slot = lax.broadcasted_iota(jnp.int32, (slots, LANES), 0)
    out_ref[...] = jnp.where(slot < cnt_ref[0], part_ref[...] + landed, 0.0)


def call(
    kernel, out_shape, n_in, scalars=0, scratch=(), n_out=1, far=(), flops=10**8, moved=10**6
):
    vmem = pl.BlockSpec(memory_space=pltpu.VMEM)
    smem = pl.BlockSpec(memory_space=pltpu.SMEM)
    hbm = pl.BlockSpec(memory_space=pltpu.HBM)
    specs = [smem] * scalars + [vmem] * (n_in - scalars + n_out)
    shapes = list(out_shape) if n_out > 1 else [out_shape]
    for place in far:
        specs[place] = hbm
        if place >= n_in:
            old = shapes[place - n_in]
            shapes[place - n_in] = pltpu.HBM(old.shape, old.dtype)
    made = pl.pallas_call(
        kernel,
        out_shape=shapes if n_out > 1 else shapes[0],
        in_specs=specs[:n_in],
        out_specs=specs[n_in:] if n_out > 1 else specs[n_in],
        scratch_shapes=list(scratch),
        compiler_params=pltpu.CompilerParams(vmem_limit_bytes=VMEM_LIMIT),
        cost_estimate=pl.CostEstimate(flops=flops, bytes_accessed=moved, transcendentals=0),
    )

    def run(*args):
        placed = [
            pltpu.with_memory_space_constraint(x, pltpu.HBM) if i in far else x
            for i, x in enumerate(args)
        ]
        return made(*placed)

    return run


def sds(shape, dtype=F32):
    return jax.ShapeDtypeStruct(shape, dtype)


def across_chips(keep, give, later):
    nb = lax.axis_size("box")
    got = lax.ppermute(give, "box", [(i, i ^ 1) for i in range(nb)])
    both, later = lax.optimization_barrier((jnp.concatenate([keep, got], axis=1), later))
    groups = [[2 * chip + (chip_side(chip) ^ g) for chip in range(nb // 2)] for g in range(2)]
    landed = lax.all_to_all(
        both, "box", split_axis=0, concat_axis=0, axis_index_groups=groups, tiled=True
    )
    return landed.reshape(nb * SEND, LANES), later


def on_device(
    multipoles, parent_locals, box_counts, box_ids, pair_source, export_slots, operators, shifters
):
    coeffs, slots = multipoles.shape
    classes = operators.shape[0]
    nb = export_slots.shape[0]
    quarters = lax.axis_size("rep")
    quarter = slots // quarters
    sent = nb * SEND
    columns = slots + sent
    heavy = 2 * classes * slots * 2 * LANES * (columns + 2 * LANES)
    ex = export_slots.T
    box = lax.axis_index("box").astype(jnp.int32)
    group = ((box & 1) ^ chip_side(box >> 1)).reshape(1)
    rep = lax.axis_index("rep").astype(jnp.int32).reshape(1)
    row = sds((slots, LANES))
    half = sds((nb // 2, SEND, LANES))
    wide = (classes, LANES, 2 * LANES)
    outgoing, mrow = call(
        export_kernel,
        [sds((sent, LANES)), row],
        2,
        n_out=2,
        far=(0, 1, 2),
        scratch=[
            pltpu.VMEM(multipoles.shape, F32),
            pltpu.VMEM(ex.shape, jnp.int32),
            pltpu.VMEM((sent, LANES), jnp.int32),
            pltpu.VMEM((sent, LANES), F32),
            pltpu.SemaphoreType.DMA,
            pltpu.SemaphoreType.DMA,
            pltpu.SemaphoreType.DMA((sent // 256,)),
        ],
    )(multipoles, ex)
    arrived = lax.all_to_all(
        outgoing.reshape(nb, SEND, LANES), "box", split_axis=0, concat_axis=0, tiled=True
    ).reshape(sent, LANES)
    w, own, keep, give = call(
        reverse_kernel,
        [sds(wide, BF), row, half, half],
        4,
        scalars=1,
        scratch=[
            pltpu.VMEM(operators.shape, F32),
            pltpu.VMEM((classes * LANES, LANES), F32),
            pltpu.VMEM(wide, BF),
            pltpu.VMEM((columns, 2 * LANES), F32),
            pltpu.SemaphoreType.DMA((classes // 8,)),
            pltpu.SemaphoreType.DMA,
        ],
        n_out=4,
        far=(1, 4),
        flops=heavy,
        moved=4 * operators.size,
    )(group, operators, mrow, pair_source)
    returned, own = across_chips(keep, give, own)
    part = call(
        forward_kernel,
        row,
        9,
        scalars=1,
        far=(1,),
        scratch=[
            pltpu.VMEM(wide, BF),
            pltpu.VMEM((columns, 2 * LANES), BF),
            pltpu.VMEM((classes, slots, LANES), jnp.int32),
            pltpu.VMEM((8 * LANES, LANES), F32),
            pltpu.VMEM((slots, 2 * LANES), F32),
            pltpu.SemaphoreType.DMA,
        ],
        flops=heavy,
        moved=4 * operators.size,
    )(rep, w, mrow, arrived, pair_source, box_ids.reshape(1, slots), parent_locals.T, shifters, own)
    summed = call(landing_kernel, row, 5, scalars=2)(group, box_counts, ex, returned, part)
    shares = lax.all_to_all(
        summed.reshape(quarters, quarter, LANES), "rep", split_axis=0, concat_axis=0, tiled=True
    )
    return jnp.sum(shares, axis=0)[:, :coeffs].T


def solution(mesh):
    return jax.shard_map(
        on_device,
        mesh=mesh,
        in_specs=(
            P(None, "box"),
            P(None, ("box", "rep")),
            P("box"),
            P("box"),
            P("rep", "box"),
            P("box", "rep"),
            P("rep", None),
            P(),
        ),
        out_specs=P(None, ("box", "rep")),
        check_vma=False,
    )
```

```python
import jax
import jax.numpy as jnp
from jax import lax
from jax.experimental import pallas as pl
from jax.experimental.pallas import tpu as pltpu
from jax.sharding import PartitionSpec as P

ORDER = 10
SEND = 8
Z_BITS = 3
LANES = 128
BF = jnp.bfloat16
F32 = jnp.float32
VMEM_LIMIT = 24 * 1024 * 1024


def mm(a, b):
    return jnp.dot(a, b, preferred_element_type=F32)


def split_hl(x):
    hi = x.astype(BF)
    lo = (x - hi.astype(F32)).astype(BF)
    return jnp.concatenate([hi, lo], axis=1)


def fold(x):
    half = x.shape[1] // 2
    return x[:, :half] + x[:, half:]


def parity_lanes(rows):
    k = lax.broadcasted_iota(jnp.int32, (rows, LANES), 1)
    degree = jnp.zeros((rows, LANES), jnp.int32)
    for level in range(1, ORDER + 1):
        degree = degree + jnp.where(k >= level * level, 1, 0)
    return jnp.where((degree & 1) == 0, 1.0, -1.0).astype(F32)


def onehot(mask):
    return jnp.where(mask, 1.0, 0.0).astype(BF)


def matrices_to_rows(src, first, coeffs, out):
    total = coeffs * coeffs
    lane = lax.broadcasted_iota(jnp.int32, (8, LANES), 1)
    for j in range(coeffs):
        base = j * coeffs // LANES * LANES
        shift = j * coeffs - base
        stop = min(base + 2 * LANES, total)
        wide = src[pl.ds(first, 8), base:stop]
        if stop < base + 2 * LANES:
            wide = jnp.concatenate([wide, jnp.zeros((8, base + 2 * LANES - stop), F32)], axis=1)
        if shift:
            wide = pltpu.roll(wide, 2 * LANES - shift, 1)
        row = jnp.where(lane < coeffs, wide[:, :LANES], 0.0)
        out[pl.ds(first * LANES + j, 8, stride=LANES), :] = row
    for j in range(coeffs, LANES):
        out[pl.ds(first * LANES + j, 8, stride=LANES), :] = jnp.zeros((8, LANES), F32)


def chip_side(chip):
    return (chip ^ (chip >> Z_BITS)) & 1


def swap_cores(ex, group):
    nb = ex.shape[1]
    lane = lax.broadcasted_iota(jnp.int32, ex.shape, 1)
    swapped = jnp.where((lane & 1) == 0, pltpu.roll(ex, nb - 1, 1), pltpu.roll(ex, 1, 1))
    return jnp.where((chip_side(lane >> 1) ^ group) == 1, swapped, ex)


def far_order(ps, slots, group):
    swapped = chip_side((ps - slots) >> 4) ^ group
    return ps ^ jnp.where(ps >= slots, SEND * swapped, 0)


def spread_rows(row, rows):
    tile = jnp.broadcast_to(row, (16, row.shape[1])).astype(F32).astype(BF)
    return jnp.concatenate([tile] * (rows // 16), axis=0)


def pick16(mask):
    return jnp.where(mask, jnp.ones((), BF), jnp.zeros((), BF))


def export_kernel(
    mult_in, ex_in, sent_ref, mrow_ref, mult_ref, ex_ref, cols_ref, mult_sem, ex_sem
):
    fetch_mult = pltpu.make_async_copy(mult_in, mult_ref, mult_sem)
    fetch_ex = pltpu.make_async_copy(ex_in, ex_ref, ex_sem)
    fetch_mult.start()
    fetch_ex.start()
    fetch_ex.wait()
    coeffs, slots = mult_ref.shape
    nb = ex_ref.shape[1]
    sent = nb * SEND
    ex = jnp.concatenate([ex_ref[...], jnp.zeros((LANES - SEND, nb), jnp.int32)], axis=0).T
    for j in range(SEND):
        cols_ref[pl.ds(j, nb, stride=SEND), :] = jnp.broadcast_to(ex[:, j : j + 1], (nb, LANES))
    fetch_mult.wait()
    wide = jnp.concatenate([mult_ref[...], jnp.zeros((LANES - coeffs, slots), F32)], axis=0)
    rows = wide.T
    mrow_ref[...] = rows
    table = split_hl(rows)
    block = 256
    lane = lax.broadcasted_iota(jnp.int32, (block, LANES), 1)
    for n in range(sent // block):
        here = pl.ds(n * block, block)
        col = cols_ref[here, :]
        hot = jnp.concatenate([onehot(lane == col - s) for s in range(0, slots, LANES)], axis=1)
        sent_ref[here, :] = fold(mm(hot, table))


def reverse_kernel(
    group_ref,
    op_in,
    mrow_ref,
    ps_in,
    w_out,
    own_ref,
    keep_ref,
    give_ref,
    op_ref,
    ps_ref,
    t_ref,
    w_ref,
    m_even,
    m_odd,
    acc_ref,
    op_sem,
    ps_sem,
    w_sem,
):
    classes = op_ref.shape[0]
    coeffs = 121
    slots = mrow_ref.shape[0]
    columns = acc_ref.shape[0]
    step = 8
    block = 256

    def fetch(k):
        rows = pl.ds(pl.multiple_of(k * 8, 8), 8)
        return pltpu.make_async_copy(op_in.at[rows, :], op_ref.at[rows, :], op_sem.at[k])

    for k in range(classes // 8):
        fetch(k).start()
    fetch_ps = pltpu.make_async_copy(ps_in, ps_ref, ps_sem)
    fetch_ps.start()

    def keep_w(g):
        part = pl.ds(g * step, step)
        return pltpu.make_async_copy(w_ref.at[part], w_out.at[part], w_sem.at[g])

    sign = parity_lanes(slots)
    moments = split_hl(mrow_ref[...] * sign)
    acc_ref[...] = jnp.zeros_like(acc_ref)
    row_id = lax.broadcasted_iota(jnp.int32, (block, slots), 0).astype(F32).astype(BF)

    def prepare(g, out):
        matrices_to_rows(op_ref, g * step, coeffs, t_ref)
        for i in range(step):
            c = g * step + i
            w = split_hl(t_ref[c * LANES : (c + 1) * LANES, :].T)
            w_ref[c] = w
            mirrored = fold(mm(moments, jnp.concatenate([w, w], axis=0)))
            out[i * slots : (i + 1) * slots, :] = split_hl(mirrored)

    def scatter(g, held):
        m = held[...]
        ps = far_order(ps_ref[g * step : (g + 1) * step, :], slots, group_ref[0])
        for start in range(0, columns, block):
            here = ps - start
            hot = jnp.concatenate(
                [pick16(row_id == spread_rows(here[i : i + 1, :], block)) for i in range(step)],
                axis=1,
            )
            acc_ref[start : start + block, :] += mm(hot, m)

    groups = classes // step
    held = (m_even, m_odd)
    fetch(0).wait()
    prepare(0, held[0])
    fetch_ps.wait()
    for g in range(1, groups):
        fetch(g).wait()
    for g in range(groups):
        keep_w(g).start()
        if g + 1 < groups:
            prepare(g + 1, held[(g + 1) % 2])
        scatter(g, held[g % 2])

    own_ref[...] = fold(acc_ref[:slots, :]) * sign
    far = columns - slots
    sums = fold(acc_ref[slots:, :]) * parity_lanes(far)
    pairs = sums.reshape(far // (2 * SEND), 2 * SEND, LANES)
    keep_ref[...] = pairs[:, :SEND, :]
    give_ref[...] = pairs[:, SEND:, :]
    for g in range(classes // step):
        keep_w(g).wait()


def forward_kernel(
    rep_ref,
    w_in,
    mrow_ref,
    arr_ref,
    ps_ref,
    ids_ref,
    par_ref,
    sh_ref,
    own_ref,
    out_ref,
    w_ref,
    table_ref,
    cols_ref,
    u_ref,
    acc_ref,
    w_sem,
):
    copy = pltpu.make_async_copy(w_in, w_ref, w_sem)
    copy.start()
    classes = w_ref.shape[0]
    slots = mrow_ref.shape[0]
    columns = table_ref.shape[0]
    coeffs = 121
    block = 256
    table_ref[:slots, :] = split_hl(mrow_ref[...])
    table_ref[slots:, :] = split_hl(arr_ref[...])
    ps = ps_ref[...]
    pst = jnp.concatenate([ps, jnp.zeros((LANES - classes, slots), jnp.int32)], axis=0).T
    for c in range(classes):
        cols_ref[c] = jnp.broadcast_to(pst[:, c : c + 1], (slots, LANES))

    acc_ref[...] = jnp.zeros_like(acc_ref)
    lane = lax.broadcasted_iota(jnp.int32, (slots, block), 1).astype(F32).astype(BF)
    group = 4
    copy.wait()

    @pl.loop(0, classes // group)
    def _(g):
        hots = []
        for i in range(group):
            col = cols_ref[g * group + i]
            parts = []
            for start in range(0, columns, block):
                here = (col - start).astype(F32).astype(BF)
                parts.append(pick16(lane == jnp.concatenate([here] * (block // LANES), axis=1)))
            hots.append(jnp.concatenate(parts, axis=1))
        picked = mm(jnp.concatenate(hots, axis=0), table_ref[...]).astype(BF)
        total = None
        for i in range(group):
            w = w_ref[g * group + i]
            part = mm(picked[i * slots : (i + 1) * slots], jnp.concatenate([w, w], axis=0))
            total = part if total is None else total + part
        acc_ref[...] += total

    matrices_to_rows(sh_ref, 0, coeffs, u_ref)
    parents = par_ref[...]
    held = parents.shape[0]
    parents = jnp.concatenate([parents, jnp.zeros((held, LANES - coeffs), F32)], axis=1)
    lhs = split_hl(parents)
    moved = []
    for o in range(8):
        w = split_hl(u_ref[o * LANES : (o + 1) * LANES, :].T)
        moved.append(fold(mm(lhs, jnp.concatenate([w, w], axis=0))))
    moved = split_hl(jnp.concatenate(moved, axis=0))
    ids = jnp.broadcast_to(ids_ref[...], (8, slots))
    parent = lax.shift_right_logical(ids, 3)
    q = parent - parent[:, 0:1] - rep_ref[0] * held
    code = jnp.where((q >= 0) & (q < held), (ids & 7) * held + q, -1)
    code = jnp.concatenate([code, jnp.zeros((LANES - 8, slots), jnp.int32)], axis=0).T
    pick = lax.broadcasted_iota(jnp.int32, (slots, 8 * held), 1)
    shifted = fold(mm(onehot(pick == code[:, 0:1]), moved))
    out_ref[...] = fold(acc_ref[...]) + own_ref[...] + shifted


def landing_kernel(group_ref, cnt_ref, ex_ref, ret_ref, part_ref, out_ref):
    slots = part_ref.shape[0]
    nb = ex_ref.shape[1]
    row = lax.broadcasted_iota(jnp.int32, (slots, nb), 0)
    ex = swap_cores(ex_ref[...], group_ref[0])
    hots = [onehot(row == ex[j : j + 1, :]) for j in range(SEND)]
    vals = [split_hl(ret_ref[pl.ds(j, nb, stride=SEND), :]) for j in range(SEND)]
    landed = fold(mm(jnp.concatenate(hots, axis=1), jnp.concatenate(vals, axis=0)))
    slot = lax.broadcasted_iota(jnp.int32, (slots, LANES), 0)
    out_ref[...] = jnp.where(slot < cnt_ref[0], part_ref[...] + landed, 0.0)


def call(
    kernel, out_shape, n_in, scalars=0, scratch=(), n_out=1, far=(), near=(), flops=10**8, moved=10**6
):
    vmem = pl.BlockSpec(memory_space=pltpu.VMEM)
    smem = pl.BlockSpec(memory_space=pltpu.SMEM)
    hbm = pl.BlockSpec(memory_space=pltpu.HBM)
    specs = [smem] * scalars + [vmem] * (n_in - scalars + n_out)
    shapes = list(out_shape) if n_out > 1 else [out_shape]
    for place in far:
        specs[place] = hbm
        if place >= n_in:
            old = shapes[place - n_in]
            shapes[place - n_in] = pltpu.HBM(old.shape, old.dtype)
    for place in near:
        old = shapes[place - n_in]
        shapes[place - n_in] = pltpu.VMEM(old.shape, old.dtype)
    made = pl.pallas_call(
        kernel,
        out_shape=shapes if n_out > 1 else shapes[0],
        in_specs=specs[:n_in],
        out_specs=specs[n_in:] if n_out > 1 else specs[n_in],
        scratch_shapes=list(scratch),
        compiler_params=pltpu.CompilerParams(vmem_limit_bytes=VMEM_LIMIT),
        cost_estimate=pl.CostEstimate(flops=flops, bytes_accessed=moved, transcendentals=0),
    )

    def run(*args):
        placed = [
            pltpu.with_memory_space_constraint(x, pltpu.HBM) if i in far else x
            for i, x in enumerate(args)
        ]
        return made(*placed)

    return run


def sds(shape, dtype=F32):
    return jax.ShapeDtypeStruct(shape, dtype)


def across_chips(keep, give, later):
    nb = lax.axis_size("box")
    got = lax.ppermute(give, "box", [(i, i ^ 1) for i in range(nb)])
    both, later = lax.optimization_barrier((jnp.concatenate([keep, got], axis=1), later))
    groups = [[2 * chip + (chip_side(chip) ^ g) for chip in range(nb // 2)] for g in range(2)]
    landed = lax.all_to_all(
        both, "box", split_axis=0, concat_axis=0, axis_index_groups=groups, tiled=True
    )
    return landed.reshape(nb * SEND, LANES), later


def on_device(
    multipoles, parent_locals, box_counts, box_ids, pair_source, export_slots, operators, shifters
):
    coeffs, slots = multipoles.shape
    classes = operators.shape[0]
    nb = export_slots.shape[0]
    quarters = lax.axis_size("rep")
    quarter = slots // quarters
    sent = nb * SEND
    columns = slots + sent
    heavy = 2 * classes * slots * 2 * LANES * (columns + 2 * LANES)
    ex = export_slots.T
    box = lax.axis_index("box").astype(jnp.int32)
    group = ((box & 1) ^ chip_side(box >> 1)).reshape(1)
    rep = lax.axis_index("rep").astype(jnp.int32).reshape(1)
    row = sds((slots, LANES))
    half = sds((nb // 2, SEND, LANES))
    wide = (classes, LANES, 2 * LANES)
    outgoing, mrow = call(
        export_kernel,
        [sds((sent, LANES)), row],
        2,
        n_out=2,
        far=(0, 1),
        near=(2,),
        scratch=[
            pltpu.VMEM(multipoles.shape, F32),
            pltpu.VMEM(ex.shape, jnp.int32),
            pltpu.VMEM((sent, LANES), jnp.int32),
            pltpu.SemaphoreType.DMA,
            pltpu.SemaphoreType.DMA,
        ],
    )(multipoles, ex)
    arrived = lax.all_to_all(
        outgoing.reshape(nb, SEND, LANES), "box", split_axis=0, concat_axis=0, tiled=True
    ).reshape(sent, LANES)
    w, own, keep, give = call(
        reverse_kernel,
        [sds(wide, BF), row, half, half],
        4,
        scalars=1,
        scratch=[
            pltpu.VMEM(operators.shape, F32),
            pltpu.VMEM((classes, slots), jnp.int32),
            pltpu.VMEM((classes * LANES, LANES), F32),
            pltpu.VMEM(wide, BF),
            pltpu.VMEM((8 * slots, 2 * LANES), BF),
            pltpu.VMEM((8 * slots, 2 * LANES), BF),
            pltpu.VMEM((columns, 2 * LANES), F32),
            pltpu.SemaphoreType.DMA((classes // 8,)),
            pltpu.SemaphoreType.DMA,
            pltpu.SemaphoreType.DMA((classes // 8,)),
        ],
        n_out=4,
        far=(1, 3, 4),
        flops=heavy,
        moved=4 * operators.size,
    )(group, operators, mrow, pair_source)
    returned, own = across_chips(keep, give, own)
    part = call(
        forward_kernel,
        row,
        9,
        scalars=1,
        far=(1,),
        scratch=[
            pltpu.VMEM(wide, BF),
            pltpu.VMEM((columns, 2 * LANES), BF),
            pltpu.VMEM((classes, slots, LANES), jnp.int32),
            pltpu.VMEM((8 * LANES, LANES), F32),
            pltpu.VMEM((slots, 2 * LANES), F32),
            pltpu.SemaphoreType.DMA,
        ],
        flops=heavy,
        moved=4 * operators.size,
    )(rep, w, mrow, arrived, pair_source, box_ids.reshape(1, slots), parent_locals.T, shifters, own)
    summed = call(landing_kernel, row, 5, scalars=2)(group, box_counts, ex, returned, part)
    shares = lax.all_to_all(
        summed.reshape(quarters, quarter, LANES), "rep", split_axis=0, concat_axis=0, tiled=True
    )
    return jnp.sum(shares, axis=0)[:, :coeffs].T


def solution(mesh):
    return jax.shard_map(
        on_device,
        mesh=mesh,
        in_specs=(
            P(None, "box"),
            P(None, ("box", "rep")),
            P("box"),
            P("box"),
            P("rep", "box"),
            P("box", "rep"),
            P("rep", None),
            P(),
        ),
        out_specs=P(None, ("box", "rep")),
        check_vma=False,
    )
```

```python
import jax
import jax.numpy as jnp
from jax import lax
from jax.experimental import pallas as pl
from jax.experimental.pallas import tpu as pltpu
from jax.sharding import PartitionSpec as P

ORDER = 10
SEND = 8
Z_BITS = 3
LANES = 128
BF = jnp.bfloat16
F32 = jnp.float32
VMEM_LIMIT = 24 * 1024 * 1024


def mm(a, b):
    return jnp.dot(a, b, preferred_element_type=F32)


def split_hl(x):
    hi = x.astype(BF)
    lo = (x - hi.astype(F32)).astype(BF)
    return jnp.concatenate([hi, lo], axis=1)


def fold(x):
    half = x.shape[1] // 2
    return x[:, :half] + x[:, half:]


def parity_lanes(rows):
    k = lax.broadcasted_iota(jnp.int32, (rows, LANES), 1)
    degree = jnp.zeros((rows, LANES), jnp.int32)
    for level in range(1, ORDER + 1):
        degree = degree + jnp.where(k >= level * level, 1, 0)
    return jnp.where((degree & 1) == 0, 1.0, -1.0).astype(F32)


def onehot(mask):
    return jnp.where(mask, 1.0, 0.0).astype(BF)


def matrices_to_rows(src, first, coeffs, out):
    total = coeffs * coeffs
    lane = lax.broadcasted_iota(jnp.int32, (8, LANES), 1)
    for j in range(coeffs):
        base = j * coeffs // LANES * LANES
        shift = j * coeffs - base
        stop = min(base + 2 * LANES, total)
        wide = src[pl.ds(first, 8), base:stop]
        if stop < base + 2 * LANES:
            wide = jnp.concatenate([wide, jnp.zeros((8, base + 2 * LANES - stop), F32)], axis=1)
        if shift:
            wide = pltpu.roll(wide, 2 * LANES - shift, 1)
        row = jnp.where(lane < coeffs, wide[:, :LANES], 0.0)
        out[pl.ds(first * LANES + j, 8, stride=LANES), :] = row
    for j in range(coeffs, LANES):
        out[pl.ds(first * LANES + j, 8, stride=LANES), :] = jnp.zeros((8, LANES), F32)


def chip_side(chip):
    return (chip ^ (chip >> Z_BITS)) & 1


def swap_cores(ex, group):
    nb = ex.shape[1]
    lane = lax.broadcasted_iota(jnp.int32, ex.shape, 1)
    swapped = jnp.where((lane & 1) == 0, pltpu.roll(ex, nb - 1, 1), pltpu.roll(ex, 1, 1))
    return jnp.where((chip_side(lane >> 1) ^ group) == 1, swapped, ex)


def far_order(ps, slots, group):
    swapped = chip_side((ps - slots) >> 4) ^ group
    return ps ^ jnp.where(ps >= slots, SEND * swapped, 0)


def spread_rows(row, rows):
    tile = jnp.broadcast_to(row, (16, row.shape[1])).astype(F32).astype(BF)
    return jnp.concatenate([tile] * (rows // 16), axis=0)


def pick16(mask):
    return jnp.where(mask, jnp.ones((), BF), jnp.zeros((), BF))


def export_kernel(
    mult_in, ex_in, sent_ref, mrow_ref, mult_ref, ex_ref, cols_ref, mult_sem, ex_sem
):
    fetch_mult = pltpu.make_async_copy(mult_in, mult_ref, mult_sem)
    fetch_ex = pltpu.make_async_copy(ex_in, ex_ref, ex_sem)
    fetch_mult.start()
    fetch_ex.start()
    fetch_ex.wait()
    coeffs, slots = mult_ref.shape
    nb = ex_ref.shape[1]
    sent = nb * SEND
    ex = jnp.concatenate([ex_ref[...], jnp.zeros((LANES - SEND, nb), jnp.int32)], axis=0).T
    for j in range(SEND):
        cols_ref[pl.ds(j, nb, stride=SEND), :] = jnp.broadcast_to(ex[:, j : j + 1], (nb, LANES))
    fetch_mult.wait()
    wide = jnp.concatenate([mult_ref[...], jnp.zeros((LANES - coeffs, slots), F32)], axis=0)
    rows = wide.T
    mrow_ref[...] = rows
    table = split_hl(rows)
    block = 256
    lane = lax.broadcasted_iota(jnp.int32, (block, LANES), 1)
    for n in range(sent // block):
        here = pl.ds(n * block, block)
        col = cols_ref[here, :]
        hot = jnp.concatenate([onehot(lane == col - s) for s in range(0, slots, LANES)], axis=1)
        sent_ref[here, :] = fold(mm(hot, table))


def reverse_kernel(
    group_ref,
    op_in,
    mrow_ref,
    ps_in,
    w_out,
    own_ref,
    keep_ref,
    give_ref,
    op_ref,
    ps_ref,
    t_ref,
    w_ref,
    m_even,
    m_odd,
    acc_ref,
    op_sem,
    ps_sem,
    w_sem,
):
    classes = op_ref.shape[0]
    coeffs = 121
    slots = mrow_ref.shape[0]
    columns = acc_ref.shape[0]
    step = 8
    block = 256

    def fetch(k):
        rows = pl.ds(pl.multiple_of(k * 8, 8), 8)
        return pltpu.make_async_copy(op_in.at[rows, :], op_ref.at[rows, :], op_sem.at[k])

    for k in range(classes // 8):
        fetch(k).start()
    fetch_ps = pltpu.make_async_copy(ps_in, ps_ref, ps_sem)
    fetch_ps.start()

    def keep_w(g):
        part = pl.ds(g * step, step)
        return pltpu.make_async_copy(w_ref.at[part], w_out.at[part], w_sem.at[g])

    sign = parity_lanes(slots)
    moments = split_hl(mrow_ref[...] * sign)
    groups = classes // step
    row_id = lax.broadcasted_iota(jnp.int32, (block, slots), 0).astype(F32).astype(BF)

    def prepare(g, out):
        matrices_to_rows(op_ref, g * step, coeffs, t_ref)
        for i in range(step):
            c = g * step + i
            w = split_hl(t_ref[c * LANES : (c + 1) * LANES, :].T)
            w_ref[c] = w
            mirrored = fold(mm(moments, jnp.concatenate([w, w], axis=0)))
            out[i * slots : (i + 1) * slots, :] = split_hl(mirrored)

    def scatter(g, held):
        m = held[...]
        ps = far_order(ps_ref[g * step : (g + 1) * step, :], slots, group_ref[0])
        for start in range(0, columns, block):
            here = ps - start
            hot = jnp.concatenate(
                [pick16(row_id == spread_rows(here[i : i + 1, :], block)) for i in range(step)],
                axis=1,
            )
            total = mm(hot, m)
            if g > 0:
                total = acc_ref[start : start + block, :] + total
            if g + 1 < groups:
                acc_ref[start : start + block, :] = total
                continue
            sums = fold(total) * sign
            if start == 0:
                own_ref[...] = sums
            else:
                pairs = sums.reshape(block // (2 * SEND), 2 * SEND, LANES)
                chips = slice((start - slots) // (2 * SEND), (start - slots + block) // (2 * SEND))
                keep_ref[chips, :, :] = pairs[:, :SEND, :]
                give_ref[chips, :, :] = pairs[:, SEND:, :]

    held = (m_even, m_odd)
    fetch(0).wait()
    prepare(0, held[0])
    fetch_ps.wait()
    for g in range(1, groups):
        fetch(g).wait()
    for g in range(groups):
        keep_w(g).start()
        if g + 1 < groups:
            prepare(g + 1, held[(g + 1) % 2])
        scatter(g, held[g % 2])

    for g in range(classes // step):
        keep_w(g).wait()


def forward_kernel(
    rep_ref,
    w_in,
    mrow_ref,
    arr_ref,
    ps_ref,
    ids_ref,
    par_ref,
    sh_ref,
    own_ref,
    out_ref,
    w_ref,
    table_ref,
    cols_ref,
    u_ref,
    acc_ref,
    w_sem,
):
    copy = pltpu.make_async_copy(w_in, w_ref, w_sem)
    copy.start()
    classes = w_ref.shape[0]
    slots = mrow_ref.shape[0]
    columns = table_ref.shape[0]
    coeffs = 121
    block = 256
    table_ref[:slots, :] = split_hl(mrow_ref[...])
    table_ref[slots:, :] = split_hl(arr_ref[...])
    ps = ps_ref[...]
    pst = jnp.concatenate([ps, jnp.zeros((LANES - classes, slots), jnp.int32)], axis=0).T
    for c in range(classes):
        cols_ref[c] = jnp.broadcast_to(pst[:, c : c + 1], (slots, LANES))

    acc_ref[...] = jnp.zeros_like(acc_ref)
    lane = lax.broadcasted_iota(jnp.int32, (slots, block), 1).astype(F32).astype(BF)
    group = 4
    copy.wait()

    @pl.loop(0, classes // group)
    def _(g):
        hots = []
        for i in range(group):
            col = cols_ref[g * group + i]
            parts = []
            for start in range(0, columns, block):
                here = (col - start).astype(F32).astype(BF)
                parts.append(pick16(lane == jnp.concatenate([here] * (block // LANES), axis=1)))
            hots.append(jnp.concatenate(parts, axis=1))
        picked = mm(jnp.concatenate(hots, axis=0), table_ref[...]).astype(BF)
        total = None
        for i in range(group):
            w = w_ref[g * group + i]
            part = mm(picked[i * slots : (i + 1) * slots], jnp.concatenate([w, w], axis=0))
            total = part if total is None else total + part
        acc_ref[...] += total

    matrices_to_rows(sh_ref, 0, coeffs, u_ref)
    parents = par_ref[...]
    held = parents.shape[0]
    parents = jnp.concatenate([parents, jnp.zeros((held, LANES - coeffs), F32)], axis=1)
    lhs = split_hl(parents)
    moved = []
    for o in range(8):
        w = split_hl(u_ref[o * LANES : (o + 1) * LANES, :].T)
        moved.append(fold(mm(lhs, jnp.concatenate([w, w], axis=0))))
    moved = split_hl(jnp.concatenate(moved, axis=0))
    ids = jnp.broadcast_to(ids_ref[...], (8, slots))
    parent = lax.shift_right_logical(ids, 3)
    q = parent - parent[:, 0:1] - rep_ref[0] * held
    code = jnp.where((q >= 0) & (q < held), (ids & 7) * held + q, -1)
    code = jnp.concatenate([code, jnp.zeros((LANES - 8, slots), jnp.int32)], axis=0).T
    pick = lax.broadcasted_iota(jnp.int32, (slots, 8 * held), 1)
    shifted = fold(mm(onehot(pick == code[:, 0:1]), moved))
    out_ref[...] = fold(acc_ref[...]) + own_ref[...] + shifted


def landing_kernel(group_ref, cnt_ref, ex_ref, ret_ref, part_ref, out_ref):
    slots = part_ref.shape[0]
    nb = ex_ref.shape[1]
    row = lax.broadcasted_iota(jnp.int32, (slots, nb), 0)
    ex = swap_cores(ex_ref[...], group_ref[0])
    hots = [onehot(row == ex[j : j + 1, :]) for j in range(SEND)]
    vals = [split_hl(ret_ref[pl.ds(j, nb, stride=SEND), :]) for j in range(SEND)]
    landed = fold(mm(jnp.concatenate(hots, axis=1), jnp.concatenate(vals, axis=0)))
    slot = lax.broadcasted_iota(jnp.int32, (slots, LANES), 0)
    out_ref[...] = jnp.where(slot < cnt_ref[0], part_ref[...] + landed, 0.0)


def call(
    kernel, out_shape, n_in, scalars=0, scratch=(), n_out=1, far=(), near=(), flops=10**8, moved=10**6
):
    vmem = pl.BlockSpec(memory_space=pltpu.VMEM)
    smem = pl.BlockSpec(memory_space=pltpu.SMEM)
    hbm = pl.BlockSpec(memory_space=pltpu.HBM)
    specs = [smem] * scalars + [vmem] * (n_in - scalars + n_out)
    shapes = list(out_shape) if n_out > 1 else [out_shape]
    for place in far:
        specs[place] = hbm
        if place >= n_in:
            old = shapes[place - n_in]
            shapes[place - n_in] = pltpu.HBM(old.shape, old.dtype)
    for place in near:
        old = shapes[place - n_in]
        shapes[place - n_in] = pltpu.VMEM(old.shape, old.dtype)
    made = pl.pallas_call(
        kernel,
        out_shape=shapes if n_out > 1 else shapes[0],
        in_specs=specs[:n_in],
        out_specs=specs[n_in:] if n_out > 1 else specs[n_in],
        scratch_shapes=list(scratch),
        compiler_params=pltpu.CompilerParams(vmem_limit_bytes=VMEM_LIMIT),
        cost_estimate=pl.CostEstimate(flops=flops, bytes_accessed=moved, transcendentals=0),
    )

    def run(*args):
        placed = [
            pltpu.with_memory_space_constraint(x, pltpu.HBM) if i in far else x
            for i, x in enumerate(args)
        ]
        return made(*placed)

    return run


def sds(shape, dtype=F32):
    return jax.ShapeDtypeStruct(shape, dtype)


def across_chips(keep, give, later):
    nb = lax.axis_size("box")
    got = lax.ppermute(give, "box", [(i, i ^ 1) for i in range(nb)])
    both, later = lax.optimization_barrier((jnp.concatenate([keep, got], axis=1), later))
    groups = [[2 * chip + (chip_side(chip) ^ g) for chip in range(nb // 2)] for g in range(2)]
    landed = lax.all_to_all(
        both, "box", split_axis=0, concat_axis=0, axis_index_groups=groups, tiled=True
    )
    return landed.reshape(nb * SEND, LANES), later


def on_device(
    multipoles, parent_locals, box_counts, box_ids, pair_source, export_slots, operators, shifters
):
    coeffs, slots = multipoles.shape
    classes = operators.shape[0]
    nb = export_slots.shape[0]
    quarters = lax.axis_size("rep")
    quarter = slots // quarters
    sent = nb * SEND
    columns = slots + sent
    heavy = 2 * classes * slots * 2 * LANES * (columns + 2 * LANES)
    ex = export_slots.T
    box = lax.axis_index("box").astype(jnp.int32)
    group = ((box & 1) ^ chip_side(box >> 1)).reshape(1)
    rep = lax.axis_index("rep").astype(jnp.int32).reshape(1)
    row = sds((slots, LANES))
    half = sds((nb // 2, SEND, LANES))
    wide = (classes, LANES, 2 * LANES)
    outgoing, mrow = call(
        export_kernel,
        [sds((sent, LANES)), row],
        2,
        n_out=2,
        far=(0, 1),
        near=(2,),
        scratch=[
            pltpu.VMEM(multipoles.shape, F32),
            pltpu.VMEM(ex.shape, jnp.int32),
            pltpu.VMEM((sent, LANES), jnp.int32),
            pltpu.SemaphoreType.DMA,
            pltpu.SemaphoreType.DMA,
        ],
    )(multipoles, ex)
    arrived = lax.all_to_all(
        outgoing.reshape(nb, SEND, LANES), "box", split_axis=0, concat_axis=0, tiled=True
    ).reshape(sent, LANES)
    w, own, keep, give = call(
        reverse_kernel,
        [sds(wide, BF), row, half, half],
        4,
        scalars=1,
        scratch=[
            pltpu.VMEM(operators.shape, F32),
            pltpu.VMEM((classes, slots), jnp.int32),
            pltpu.VMEM((classes * LANES, LANES), F32),
            pltpu.VMEM(wide, BF),
            pltpu.VMEM((8 * slots, 2 * LANES), BF),
            pltpu.VMEM((8 * slots, 2 * LANES), BF),
            pltpu.VMEM((columns, 2 * LANES), F32),
            pltpu.SemaphoreType.DMA((classes // 8,)),
            pltpu.SemaphoreType.DMA,
            pltpu.SemaphoreType.DMA((classes // 8,)),
        ],
        n_out=4,
        far=(1, 3, 4),
        flops=heavy,
        moved=4 * operators.size,
    )(group, operators, mrow, pair_source)
    returned, own = across_chips(keep, give, own)
    part = call(
        forward_kernel,
        row,
        9,
        scalars=1,
        far=(1,),
        scratch=[
            pltpu.VMEM(wide, BF),
            pltpu.VMEM((columns, 2 * LANES), BF),
            pltpu.VMEM((classes, slots, LANES), jnp.int32),
            pltpu.VMEM((8 * LANES, LANES), F32),
            pltpu.VMEM((slots, 2 * LANES), F32),
            pltpu.SemaphoreType.DMA,
        ],
        flops=heavy,
        moved=4 * operators.size,
    )(rep, w, mrow, arrived, pair_source, box_ids.reshape(1, slots), parent_locals.T, shifters, own)
    summed = call(landing_kernel, row, 5, scalars=2)(group, box_counts, ex, returned, part)
    shares = lax.all_to_all(
        summed.reshape(quarters, quarter, LANES), "rep", split_axis=0, concat_axis=0, tiled=True
    )
    return jnp.sum(shares, axis=0)[:, :coeffs].T


def solution(mesh):
    return jax.shard_map(
        on_device,
        mesh=mesh,
        in_specs=(
            P(None, "box"),
            P(None, ("box", "rep")),
            P("box"),
            P("box"),
            P("rep", "box"),
            P("box", "rep"),
            P("rep", None),
            P(),
        ),
        out_specs=P(None, ("box", "rep")),
        check_vma=False,
    )
```
